512 devices in a mesh: dp: 16 (over x, y), ctx: 32 (over z, core).
Axes of the slice: x: 4, y: 4, z: 16, core: 2. Of those that a mesh axis runs over, the one named last changes fastest.
Arguments:
- queries: bfloat16 [65536, 3072], P(('dp', 'ctx')), parts along dimension 0
- key_vectors: bfloat16 [65536, 512], P(('dp', 'ctx')), parts along dimension 0
- value_vectors: bfloat16 [65536, 512], P(('dp', 'ctx')), parts along dimension 0, may hold values from -6 to 6
- d_output: bfloat16 [65536, 3072], P(('dp', 'ctx')), parts along dimension 0, may hold values from -6 to 6
- doc_blocks: int32 [256], P('dp'), parts along dimension 0, may hold values from 1 to 4, 32 in all
Outputs:
- d_queries: bfloat16 [65536, 3072], P(('dp', 'ctx')), parts along dimension 0
- d_keys: bfloat16 [65536, 512], P(('dp', 'ctx')), parts along dimension 0
- d_values: bfloat16 [65536, 512], P(('dp', 'ctx')), parts along dimension 0
The draws below stay inside these ranges and needn't reach their ends.
There are 16 independent parts, one for each index of `dp`. The reference program is written for one: setup_inputs(seed, part) draws one part's arguments, and reference() takes and returns one part's arrays. A program takes and returns all parts, laid end to end along the dimension named above; each array names one. Nothing has to cross between parts.
Inputs may be any that keep to these rules, and one draw needn't show every extreme that they name: `doc_blocks`: 16 documents that fill the pack exactly: the lengths sum to 32, and the longest is exactly 4.
All inputs are finite; a program needn't handle non-finite values.
Results may differ from the reference program's by a relative error of at most 0.011.
Values may be sent and summed in bfloat16 or wider, within the bound.
A program may use at most 64 MiB of HBM per device.

```python
import math
import jax
import jax.numpy as jnp
import numpy as np
from jax import lax

QH = 24
KVH = 4
HD = 128
TOK_DEV = 128
BLOCK = 128
SPAN = 4
TOKENS = 4096
NDOCS = 16
N_CTX = 32


def common_keys(key):
    return jax.random.normal(key, (TOKENS, KVH, HD), jnp.float32)


def draw_key_vectors(key, part):
    common = common_keys(key)
    return common.reshape(TOKENS, KVH * HD).astype(jnp.bfloat16)


def draw_queries(key, part):
    key = jax.random.fold_in(key, 5)
    normals = jax.random.normal(key, (TOKENS, QH, HD), jnp.float32)
    return normals.reshape(TOKENS, QH * HD).astype(jnp.bfloat16)


def steps_of(rng, dims, cuts, least, largest):
    def one(dim, parts):
        steps = jax.random.uniform(jax.random.fold_in(jax.random.fold_in(rng, 6), dim), (parts,), jnp.float32, least / len(cuts), largest / len(cuts))
        return jnp.repeat(jnp.exp(steps), dims[dim] // parts).reshape((-1,) + (1,) * (len(dims) - dim - 1))

    level = one(*cuts[0])
    for cut in cuts[1:]:
        level = level * one(*cut)
    return level


def split_up(amount, total, most, skew):
    loads = [(1 << 20) // math.isqrt(standing ** skew) + 1 for standing in range(2, amount + 1)]
    surplus, holding = total - most - (amount - 1), [1] * (amount - 1)
    while surplus > 0:
        candidates = [i for i in range(amount - 1) if holding[i] < most]
        whole, remaining = sum([loads[i] for i in candidates]), surplus
        for i in candidates:
            addition = min(most - holding[i], max(1, remaining * loads[i] // whole), surplus)
            holding[i] = holding[i] + addition
            surplus = surplus - addition
    return np.array([most] + holding)


def uneven_parts(rng, number_of, total, limit, slope):
    if number_of == 2:
        one = jax.random.randint(rng, (), max(1, total - limit), min(limit, total - 1) + 1)
        return jnp.stack([one, total - one])
    sizes = jnp.asarray(split_up(number_of, total, limit, slope), jnp.int32)
    twos = (number_of - 1) // 2
    source_of, sink = sizes[1:1 + 2 * twos:2], sizes[2:2 + 2 * twos:2]
    room = jnp.minimum(source_of - 1, limit - sink)
    passed = jax.random.randint(jax.random.fold_in(rng, 1), (twos,), 0, 1 << 20) % (room + 1)
    sizes = sizes.at[1:1 + 2 * twos:2].set(source_of - passed).at[2:2 + 2 * twos:2].set(sink + passed)
    return sizes[jax.random.permutation(jax.random.fold_in(rng, 2), number_of)]


def bell_draw(rng, extent, deviation, reach, shards=(), held_as=jnp.bfloat16):
    array = jax.random.normal(rng, extent, jnp.float32) * deviation
    if len(shards) > 0:
        array = steps_of(rng, extent, shards, -0.22, 0.18) * array
    return jnp.clip(array, min=-reach, max=reach).astype(held_as)


def setup_inputs(seed: int = 0, part: int = 0) -> dict:
    keys = jax.random.split(jax.random.key(seed), 6)
    part_splits = jax.random.split(jax.random.fold_in(keys[5], part), 6)
    return {
        "queries": draw_queries(jax.random.fold_in(jax.random.fold_in(keys[5], part), 71), part),
        "key_vectors": draw_key_vectors(jax.random.fold_in(jax.random.fold_in(keys[5], part), 71), part),
        "value_vectors": bell_draw(part_splits[2], (TOKENS, KVH * HD), 1.0, 6.0, ((0, 32),)),
        "d_output": bell_draw(part_splits[3], (TOKENS, QH * HD), 1.0, 6.0, ((0, 32),)),
        "doc_blocks": uneven_parts(part_splits[4], NDOCS, TOKENS // BLOCK, SPAN * TOK_DEV // BLOCK, 2).astype(jnp.int32),
    }


def doc_of(positions, doc_blocks):
    doc_ends = jnp.cumsum(doc_blocks).astype(jnp.int32) * BLOCK
    return lax.optimization_barrier(jnp.sum((positions[:, None] >= doc_ends[None, :]).astype(jnp.int32), axis=1))

def reference(queries, key_vectors, value_vectors, d_output, doc_blocks):
    per_group = QH // KVH
    inv_root = 1.0 / math.sqrt(HD)
    key_rows = (SPAN + 1) * TOK_DEV
    padding = SPAN * TOK_DEV
    keys_pad = jnp.concatenate([jnp.zeros((padding, KVH, HD), jnp.bfloat16), key_vectors.reshape(TOKENS, KVH, HD)], 0)
    values_pad = jnp.concatenate([jnp.zeros((padding, KVH, HD), jnp.bfloat16), value_vectors.reshape(TOKENS, KVH, HD)], 0)

    def one_block(carry, block_index):
        sum_keys, sum_values = carry
        first_row = (block_index * TOK_DEV).astype(jnp.int32)
        query_grp = lax.dynamic_slice_in_dim(queries, first_row, TOK_DEV, 0).reshape(TOK_DEV, KVH, per_group, HD).astype(jnp.float32)
        dout_grp = lax.dynamic_slice_in_dim(d_output, first_row, TOK_DEV, 0).reshape(TOK_DEV, KVH, per_group, HD).astype(jnp.float32)
        key_grp = lax.dynamic_slice_in_dim(keys_pad, first_row, key_rows, 0).astype(jnp.float32)
        value_grp = lax.dynamic_slice_in_dim(values_pad, first_row, key_rows, 0).astype(jnp.float32)
        query_pos = first_row + jnp.arange(TOK_DEV, dtype=jnp.int32)
        key_pos = first_row - padding + jnp.arange(key_rows, dtype=jnp.int32)
        allowed = doc_of(key_pos, doc_blocks)[None, :] == doc_of(query_pos, doc_blocks)[:, None]
        allowed = allowed & (key_pos[None, :] <= query_pos[:, None]) & (key_pos[None, :] >= 0)
        scores = jnp.einsum('tgja,uga->gjtu', query_grp, key_grp) * inv_root
        scores = jnp.where(allowed[None, None], scores, -jnp.inf)
        top_score = lax.optimization_barrier(jnp.max(scores, axis=-1, keepdims=True))
        probs = jnp.exp(scores - top_score)
        probs = probs / lax.optimization_barrier(jnp.sum(probs, axis=-1, keepdims=True))
        probs_low = lax.optimization_barrier(probs.astype(jnp.bfloat16)).astype(jnp.float32)
        attended = jnp.einsum('gjtu,uga->tgja', probs_low, value_grp)
        row_delta = jnp.transpose(lax.optimization_barrier(jnp.sum(dout_grp * attended, axis=-1)), (1, 2, 0))
        dprobs = jnp.einsum('tgja,uga->gjtu', dout_grp, value_grp)
        dscores = probs * (dprobs - row_delta[..., None])
        dscores_low = lax.optimization_barrier(dscores.astype(jnp.bfloat16)).astype(jnp.float32)
        dquery = (jnp.einsum('gjtu,uga->tgja', dscores_low, key_grp) * inv_root).astype(jnp.bfloat16)
        key_term = (jnp.einsum('gjtu,tgja->uga', dscores_low, query_grp) * inv_root).astype(jnp.bfloat16)
        value_term = jnp.einsum('gjtu,tgja->uga', probs_low, dout_grp).astype(jnp.bfloat16)
        key_term = lax.optimization_barrier(key_term).astype(jnp.float32)
        value_term = lax.optimization_barrier(value_term).astype(jnp.float32)
        sum_keys = lax.dynamic_update_slice_in_dim(sum_keys, lax.dynamic_slice_in_dim(sum_keys, first_row, key_rows, 0) + key_term, first_row, 0)
        sum_values = lax.dynamic_update_slice_in_dim(sum_values, lax.dynamic_slice_in_dim(sum_values, first_row, key_rows, 0) + value_term, first_row, 0)
        return ((sum_keys, sum_values), dquery.reshape(TOK_DEV, QH * HD))
    start_sums = (jnp.zeros((padding + TOKENS, KVH, HD), jnp.float32), jnp.zeros((padding + TOKENS, KVH, HD), jnp.float32))
    (sum_keys, sum_values), dquery = lax.scan(one_block, start_sums, jnp.arange(N_CTX, dtype=jnp.int32))
    d_queries = dquery.reshape(TOKENS, QH * HD)
    d_keys = sum_keys[padding:].reshape(TOKENS, KVH * HD).astype(jnp.bfloat16)
    d_values = sum_values[padding:].reshape(TOKENS, KVH * HD).astype(jnp.bfloat16)
    return (d_queries, d_keys, d_values)
```

```python
import functools
import math

import jax
import jax.numpy as jnp
from jax import lax
from jax.experimental import pallas as pl
from jax.experimental.pallas import tpu as pltpu
from jax.sharding import PartitionSpec as P

QH = 24
KVH = 4
HD = 128
PER = QH // KVH
ROWS = 128
SPAN = 4
NDOCS = 16
WIDE = PER * HD
PAIRS = PER // 2
INV_ROOT = 1.0 / math.sqrt(HD)
EXP2_SCALE = INV_ROOT * math.log2(math.e)
MESH = pl.DeviceIdType.MESH
NT = (((1,), (1,)), ((), ()))
NN = (((1,), (0,)), ((), ()))
KEYS = SPAN * ROWS


def dot(a, b, dims):
    return lax.dot_general(a, b, dims, preferred_element_type=jnp.float32)


def kernel(
    n_ctx,
    docs,
    q_hbm,
    k_hbm,
    v_hbm,
    do_hbm,
    dq_hbm,
    dk_out,
    dv_out,
    q_v,
    do_v,
    dq_v,
    kv,
    k_t,
    p_s,
    ds_s,
    terms,
    own_terms,
    sums,
    back,
    load_sem,
    kv_sem,
    store_sem,
    send_sem,
    recv_sem,
    back_send,
    back_recv,
):
    me = lax.axis_index("ctx")
    core = lax.rem(me, 2)
    chip = lax.div(me, 2)
    chips = n_ctx // 2
    nxt = lax.rem(chip + 1, chips) * 2
    prv = lax.rem(chip + chips - 1, chips) * 2
    sibling = chip * 2 + (1 - core)
    cross_next = nxt + (1 - core)
    cross_prev = prv + (1 - core)
    is_even = core == 0

    def kv_load(g, which):
        src = (k_hbm, v_hbm)[which]
        return pltpu.make_async_copy(
            src.at[:, g * HD : (g + 1) * HD], kv.at[g, which, 0:ROWS], kv_sem.at[g, which]
        )

    for g in range(KVH):
        for which in range(2):
            kv_load(g, which).start()

    def q_load(g):
        cols = slice(g * WIDE, (g + 1) * WIDE)
        return (
            pltpu.make_async_copy(q_hbm.at[:, cols], q_v.at[g], load_sem.at[g, 0]),
            pltpu.make_async_copy(do_hbm.at[:, cols], do_v.at[g], load_sem.at[g, 1]),
        )

    for g in range(KVH):
        for copy in q_load(g):
            copy.start()

    barrier = pltpu.get_barrier_semaphore()

    def greet(device):
        pl.semaphore_signal(barrier, inc=1, device_id={"ctx": device}, device_id_type=MESH)

    greet(sibling)
    greet(cross_next)
    greet(cross_prev)

    @pl.when(is_even)
    def _():
        greet(nxt)
        greet(prv)

    end = jnp.int32(0)
    start = jnp.int32(0)
    for i in range(NDOCS):
        end = end + docs[i]
        start = jnp.where(end <= me, end, start)
    inside = [me - d >= start for d in range(SPAN)]

    for g in range(KVH):
        for which in range(2):
            kv_load(g, which).wait()

    @pl.when(is_even)
    def _():
        pl.semaphore_wait(barrier, 5)

    @pl.when(core == 1)
    def _():
        pl.semaphore_wait(barrier, 3)

    def kv_copy(g, from_slot, to_slot, kind, device):
        return pltpu.make_async_remote_copy(
            src_ref=kv.at[g, :, pl.ds(pl.multiple_of(from_slot * ROWS, ROWS), ROWS)],
            dst_ref=kv.at[g, :, pl.ds(pl.multiple_of(to_slot * ROWS, ROWS), ROWS)],
            send_sem=send_sem.at[kind, g],
            recv_sem=recv_sem.at[to_slot, g],
            device_id={"ctx": device},
            device_id_type=MESH,
        )

    cross_slot = 3 - 2 * core
    relay_slot = 1 + 2 * core

    def own_cross(g):
        return kv_copy(g, 0, cross_slot, 0, cross_next)

    def own_sibling(g):
        return kv_copy(g, 0, 1, 1, sibling)

    def relay_sibling(g):
        return kv_copy(g, relay_slot, 2, 2, sibling)

    def relay_cross(g):
        return kv_copy(g, 1, 3, 3, nxt)

    def send_own(g):
        own_cross(g).start()

        @pl.when(is_even)
        def _():
            own_sibling(g).start()

    def wait_slot(g, slot):
        kv_copy(g, 0, slot, 0, sibling).wait_recv()

    def relay(g):
        wait_slot(g, relay_slot)
        relay_sibling(g).start()

        @pl.when(is_even)
        def _():
            relay_cross(g).start()

    def back_copy(src, slot, kind, g, device):
        return pltpu.make_async_remote_copy(
            src_ref=src,
            dst_ref=back.at[slot, g],
            send_sem=back_send.at[kind, g],
            recv_sem=back_recv.at[slot, g],
            device_id={"ctx": device},
            device_id_type=MESH,
        )

    far = 3 - 2 * core
    far_device = jnp.where(is_even, prv, sibling)

    def send_near(g):
        return back_copy(terms.at[g, 1], 0, 0, g, sibling)

    def send_far(g):
        return back_copy(terms.at[g, far - 1], 3 - core, 1, g, far_device)

    def send_sum(g):
        return back_copy(sums.at[g], 1, 2, g, cross_prev)

    def wait_back(slot, g):
        back_copy(sums.at[g], slot, 2, g, sibling).wait_recv()

    def reduce(g):
        wait_back(0, g)

        @pl.when(is_even)
        def _():
            wait_back(3, g)
            for w in range(2):
                total = terms[g, 0, w].astype(jnp.float32) + back[0, g, w].astype(jnp.float32)
                sums[g, w] = (total + back[3, g, w].astype(jnp.float32)).astype(jnp.bfloat16)

        @pl.when(core == 1)
        def _():
            for w in range(2):
                total = terms[g, 2, w].astype(jnp.float32) + back[0, g, w].astype(jnp.float32)
                sums[g, w] = total.astype(jnp.bfloat16)

        send_sum(g).start()

    def finish(g):
        wait_back(1, g)

        @pl.when(is_even)
        def _():
            wait_back(2, g)
            for w in range(2):
                own_terms[g, w] += back[2, g, w].astype(jnp.float32)

        for w in range(2):
            own_terms[g, w] += back[1, g, w].astype(jnp.float32)

    later = lax.broadcasted_iota(jnp.int32, (ROWS, 2 * ROWS), 0) > lax.rem(
        lax.broadcasted_iota(jnp.int32, (ROWS, 2 * ROWS), 1), ROWS
    )

    def compute(g):
        for which in range(2):
            pltpu.make_async_copy(
                (q_v, do_v)[which].at[g], (q_v, do_v)[which].at[g], load_sem.at[g, which]
            ).wait()
        keys = kv[g, 0]
        k_t[...] = keys.T
        for pair in range(PAIRS):
            lo = pair * 2 * HD
            q2 = jnp.concatenate([q_v[g, :, lo : lo + HD], q_v[g, :, lo + HD : lo + 2 * HD]], 0)
            do2 = jnp.concatenate([do_v[g, :, lo : lo + HD], do_v[g, :, lo + HD : lo + 2 * HD]], 0)
            blocks = []
            tops = []
            for d in range(SPAN):
                k_d = kv[g, 0, d * ROWS : (d + 1) * ROWS]
                if d > 0:
                    k_d = jnp.where(inside[d], k_d, jnp.zeros_like(k_d))
                s_d = dot(k_d, q2, NT)
                if d == 0:
                    s_d = jnp.where(later, -jnp.inf, s_d)
                top = jnp.max(s_d, axis=0, keepdims=True)
                if d > 0:
                    top = jnp.where(inside[d], top, -jnp.inf)
                blocks.append(s_d)
                tops.append(top)
            top = functools.reduce(jnp.maximum, tops)
            exps = []
            norm = jnp.zeros_like(top)
            for d in range(SPAN):
                top_d = top if d == 0 else jnp.where(inside[d], top, jnp.inf)
                e_d = jnp.exp2((blocks[d] - top_d) * EXP2_SCALE)
                norm = norm + jnp.sum(e_d, axis=0, keepdims=True)
                exps.append(e_d)
            inv = 1.0 / norm
            delta = jnp.zeros_like(top)
            dps = []
            for d in range(SPAN):
                p_d = exps[d] * inv
                exps[d] = p_d
                p_s[d * ROWS : (d + 1) * ROWS, lo : lo + 2 * HD] = p_d.astype(jnp.bfloat16)
                dp_d = dot(kv[g, 1, d * ROWS : (d + 1) * ROWS], do2, NT)
                delta = delta + jnp.sum(p_d * dp_d, axis=0, keepdims=True)
                dps.append(dp_d)
            for d in range(SPAN):
                ds_d = exps[d] * (dps[d] - delta)
                ds_s[d * ROWS : (d + 1) * ROWS, lo : lo + 2 * HD] = ds_d.astype(jnp.bfloat16)
        q6 = jnp.concatenate([q_v[g, :, j * HD : (j + 1) * HD] for j in range(PER)], 0)
        do6 = jnp.concatenate([do_v[g, :, j * HD : (j + 1) * HD] for j in range(PER)], 0)
        dk = dot(ds_s[...], q6, NN) * INV_ROOT
        dv = dot(p_s[...], do6, NN)
        for w, d_w in enumerate((dk, dv)):
            own_terms[g, w] = d_w[0:ROWS]
            for d in range(1, SPAN):
                terms[g, d - 1, w] = d_w[d * ROWS : (d + 1) * ROWS].astype(jnp.bfloat16)

    def queries_out(g):
        dq_t = dot(k_t[...], ds_s[...], NN) * INV_ROOT
        for j in range(PER):
            dq_v[g, :, j * HD : (j + 1) * HD] = dq_t[:, j * HD : (j + 1) * HD].T.astype(jnp.bfloat16)

    def dq_store(g):
        return pltpu.make_async_copy(
            dq_v.at[g], dq_hbm.at[:, pl.ds(pl.multiple_of(g * WIDE, WIDE), WIDE)], store_sem.at[g]
        )

    send_own(0)
    send_own(1)
    relay(0)
    send_own(2)

    def step(g, carry):
        @pl.when(g < KVH - 1)
        def _():
            relay(g + 1)

            @pl.when(g < 1)
            def _():
                send_own(g + 3)

        wait_slot(g, 2)
        wait_slot(g, cross_slot)
        compute(g)
        send_far(g).start()
        send_near(g).start()
        queries_out(g)
        dq_store(g).start()

        @pl.when(g > 0)
        def _():
            reduce(g - 1)

        return carry

    lax.fori_loop(0, KVH, step, 0)
    for g in range(KVH - 1):
        finish(g)
    reduce(KVH - 1)
    finish(KVH - 1)
    for g in range(KVH):
        dk_out[:, g * HD : (g + 1) * HD] = own_terms[g, 0].astype(jnp.bfloat16)
        dv_out[:, g * HD : (g + 1) * HD] = own_terms[g, 1].astype(jnp.bfloat16)
    for g in range(KVH):
        own_cross(g).wait_send()
        relay_sibling(g).wait_send()
        send_near(g).wait_send()
        send_far(g).wait_send()
        send_sum(g).wait_send()
        dq_store(g).wait()

    @pl.when(is_even)
    def _():
        for g in range(KVH):
            own_sibling(g).wait_send()
            relay_cross(g).wait_send()


def solution(mesh):
    n_ctx = mesh.shape["ctx"]
    any_space = pl.BlockSpec(memory_space=pl.ANY)
    vmem = pl.BlockSpec(memory_space=pltpu.VMEM)
    bf16, f32 = jnp.bfloat16, jnp.float32

    def per_device(queries, key_vectors, value_vectors, d_output, doc_blocks):
        return pl.pallas_call(
            functools.partial(kernel, n_ctx),
            out_shape=(
                jax.ShapeDtypeStruct((ROWS, QH * HD), bf16),
                jax.ShapeDtypeStruct((ROWS, KVH * HD), bf16),
                jax.ShapeDtypeStruct((ROWS, KVH * HD), bf16),
            ),
            in_specs=[pl.BlockSpec(memory_space=pltpu.SMEM)] + [any_space] * 4,
            out_specs=(any_space, vmem, vmem),
            scratch_shapes=[
                pltpu.VMEM((KVH, ROWS, WIDE), bf16),
                pltpu.VMEM((KVH, ROWS, WIDE), bf16),
                pltpu.VMEM((KVH, ROWS, WIDE), bf16),
                pltpu.VMEM((KVH, 2, KEYS, HD), bf16),
                pltpu.VMEM((HD, KEYS), bf16),
                pltpu.VMEM((KEYS, WIDE), bf16),
                pltpu.VMEM((KEYS, WIDE), bf16),
                pltpu.VMEM((KVH, SPAN - 1, 2, ROWS, HD), bf16),
                pltpu.VMEM((KVH, 2, ROWS, HD), f32),
                pltpu.VMEM((KVH, 2, ROWS, HD), bf16),
                pltpu.VMEM((4, KVH, 2, ROWS, HD), bf16),
                pltpu.SemaphoreType.DMA((KVH, 2)),
                pltpu.SemaphoreType.DMA((KVH, 2)),
                pltpu.SemaphoreType.DMA((KVH,)),
                pltpu.SemaphoreType.DMA((4, KVH)),
                pltpu.SemaphoreType.DMA((SPAN, KVH)),
                pltpu.SemaphoreType.DMA((3, KVH)),
                pltpu.SemaphoreType.DMA((4, KVH)),
            ],
            compiler_params=pltpu.CompilerParams(
                collective_id=0, has_side_effects=True, vmem_limit_bytes=48 * 1024 * 1024
            ),
        )(doc_blocks, queries, key_vectors, value_vectors, d_output)

    spec = P(("dp", "ctx"), None)
    return jax.shard_map(
        per_device,
        mesh=mesh,
        in_specs=(spec, spec, spec, spec, P("dp")),
        out_specs=(spec, spec, spec),
        check_vma=False,
    )
```

```python
import functools
import math

import jax
import jax.numpy as jnp
from jax import lax
from jax.experimental import pallas as pl
from jax.experimental.pallas import tpu as pltpu
from jax.sharding import PartitionSpec as P

QH = 24
KVH = 4
HD = 128
PER = QH // KVH
ROWS = 128
SPAN = 4
NDOCS = 16
WIDE = PER * HD
PAIRS = PER // 2
INV_ROOT = 1.0 / math.sqrt(HD)
EXP2_SCALE = INV_ROOT * math.log2(math.e)
MESH = pl.DeviceIdType.MESH
NT = (((1,), (1,)), ((), ()))
NN = (((1,), (0,)), ((), ()))
KEYS = SPAN * ROWS
STORES = 4


def dot(a, b, dims):
    return lax.dot_general(a, b, dims, preferred_element_type=jnp.float32)


def kernel(
    n_ctx,
    docs_hbm,
    q_hbm,
    k_hbm,
    v_hbm,
    do_hbm,
    dq_out,
    dk_out,
    dv_out,
    docs,
    q_v,
    do_v,
    kv,
    k_t,
    p_s,
    ds_s,
    terms,
    own_terms,
    sums,
    back,
    docs_sem,
    load_sem,
    kv_sem,
    send_sem,
    recv_sem,
    back_send,
    back_recv,
):
    me = lax.axis_index("ctx")
    core = lax.rem(me, 2)
    chip = lax.div(me, 2)
    sibling = chip * 2 + (1 - core)
    near_slot = 1 + 2 * core
    far = 3 - 2 * core

    is_even, is_odd = core == 0, core == 1
    before, after = chip >= 1, me + 2 < n_ctx
    even_before, odd_before = is_even & before, is_odd & before
    even_after, odd_after = is_even & after, is_odd & after
    relays_on = even_before & after
    straight_from, straight_to = is_even & (chip >= 2), is_odd & (me + 3 < n_ctx)

    barrier = pltpu.get_barrier_semaphore()
    partners = (
        (me >= 0, sibling),
        (even_before, me - 1),
        (odd_after, me + 1),
        (even_after, me + 3),
        (odd_before, me - 3),
        (even_after, me + 2),
        (even_before, me - 2),
        (straight_from, me - 3),
        (straight_to, me + 3),
    )
    for there, device in partners:

        @pl.when(there)
        def _():
            pl.semaphore_signal(barrier, inc=1, device_id={"ctx": device}, device_id_type=MESH)

    docs_copy = pltpu.make_async_copy(docs_hbm, docs, docs_sem)
    docs_copy.start()

    def kv_load(g, which):
        src = (k_hbm, v_hbm)[which]
        return pltpu.make_async_copy(
            src.at[:, g * HD : (g + 1) * HD], kv.at[g, which, 0:ROWS], kv_sem.at[g, which]
        )

    for g in range(KVH):
        for which in range(2):
            kv_load(g, which).start()

    def q_load(g):
        cols = slice(g * WIDE, (g + 1) * WIDE)
        return (
            pltpu.make_async_copy(q_hbm.at[:, cols], q_v.at[g], load_sem.at[g, 0]),
            pltpu.make_async_copy(do_hbm.at[:, cols], do_v.at[g], load_sem.at[g, 1]),
        )

    for g in range(KVH):
        for copy in q_load(g):
            copy.start()

    @pl.when(me < SPAN - 1)
    def _():
        for d in range(1, SPAN):

            @pl.when(me < d)
            def _():
                kv[:, :, d * ROWS : (d + 1) * ROWS] = jnp.zeros((KVH, 2, ROWS, HD), jnp.bfloat16)

    for g in range(KVH):
        for which in range(2):
            kv_load(g, which).wait()
    docs_copy.wait()

    end = jnp.int32(0)
    start = jnp.int32(0)
    for i in range(NDOCS):
        end = end + docs[i]
        start = jnp.where(end <= me, end, start)
    inside = [me - d >= start for d in range(SPAN)]

    pl.semaphore_wait(barrier, sum(there.astype(jnp.int32) for there, _ in partners))

    def kv_copy(g, from_slot, to_slot, kind, device):
        return pltpu.make_async_remote_copy(
            src_ref=kv.at[g, :, pl.ds(pl.multiple_of(from_slot * ROWS, ROWS), ROWS)],
            dst_ref=kv.at[g, :, pl.ds(pl.multiple_of(to_slot * ROWS, ROWS), ROWS)],
            send_sem=send_sem.at[kind, g],
            recv_sem=recv_sem.at[to_slot, g],
            device_id={"ctx": device},
            device_id_type=MESH,
        )

    def own_cross(g):
        return kv_copy(g, 0, far, 0, me + far)

    def own_sibling(g):
        return kv_copy(g, 0, 1, 1, sibling)

    def pass_sibling(g):
        return kv_copy(g, near_slot, 2, 2, sibling)

    def pass_cross(g):
        return kv_copy(g, 1, 3, 3, me + 2)

    def send_cross(g):
        @pl.when(after)
        def _():
            own_cross(g).start()

    def send_sibling(g):
        @pl.when(is_even)
        def _():
            own_sibling(g).start()

    def wait_slot(g, slot, there):
        @pl.when(there)
        def _():
            kv_copy(g, 0, slot, 0, sibling).wait_recv()

    def relay(g):
        @pl.when(before)
        def _():
            kv_copy(g, 0, near_slot, 0, sibling).wait_recv()

            pass_sibling(g).start()

            @pl.when(relays_on)
            def _():
                pass_cross(g).start()

    def wait_keys(g):
        wait_slot(g, 2, before)
        wait_slot(g, far, is_odd | (chip >= 2))

    def back_copy(src, slot, kind, g, device):
        return pltpu.make_async_remote_copy(
            src_ref=src,
            dst_ref=back.at[slot, g],
            send_sem=back_send.at[kind, g],
            recv_sem=back_recv.at[slot, g],
            device_id={"ctx": device},
            device_id_type=MESH,
        )

    far_on = is_odd | (chip >= 2)

    early_sum = is_odd | jnp.logical_not(straight_from & after)

    def by_chip(g):
        return (g < KVH - 1) & (is_even & (me != 4))

    def joins(g):
        return (g < KVH - 1) & (straight_from & after)

    def send_pair(g):
        return back_copy(terms.at[g, 1], 0, 0, g, sibling)

    def send_far(g):
        slot = jnp.where(by_chip(g), 3, 2)
        device = jnp.where(by_chip(g), me - 2, me - far)
        return back_copy(terms.at[g, far - 1], slot, 1, g, device)

    def send_sum(g):
        return back_copy(sums.at[g], 1, 2, g, me - near_slot)

    def wait_back(slot, g):
        back_copy(sums.at[g], slot, 2, g, sibling).wait_recv()

    def reduce(g):
        @pl.when(before)
        def _():
            wait_back(0, g)

            @pl.when(joins(g))
            def _():
                wait_back(3, g)
                for w in range(2):
                    total = terms[g, 0, w].astype(jnp.float32) + back[0, g, w].astype(jnp.float32)
                    sums[g, w] = (total + back[3, g, w].astype(jnp.float32)).astype(jnp.bfloat16)

            @pl.when(jnp.logical_not(joins(g)))
            def _():
                for w in range(2):
                    mine = terms[g, near_slot - 1, w].astype(jnp.float32)
                    sums[g, w] = (mine + back[0, g, w].astype(jnp.float32)).astype(jnp.bfloat16)

            send_sum(g).start()

    def finish(g):
        @pl.when(is_even | (straight_to & (me == 1 if g < KVH - 1 else me >= 0)))
        def _():
            wait_back(2, g)
            for w in range(2):
                own_terms[g, w] += back[2, g, w].astype(jnp.float32)

        @pl.when(after)
        def _():
            wait_back(1, g)
            for w in range(2):
                own_terms[g, w] += back[1, g, w].astype(jnp.float32)

    later = lax.broadcasted_iota(jnp.int32, (ROWS, 2 * ROWS), 0) > lax.rem(
        lax.broadcasted_iota(jnp.int32, (ROWS, 2 * ROWS), 1), ROWS
    )

    def between(g):
        @pl.when(g < KVH - 2)
        def _():
            relay(g + 2)

        @pl.when((g > 0) & early_sum)
        def _():
            reduce(g - 1)

    def compute(g):
        for which in range(2):
            pltpu.make_async_copy(
                (q_v, do_v)[which].at[g], (q_v, do_v)[which].at[g], load_sem.at[g, which]
            ).wait()
        keys = kv[g, 0]
        k_t[...] = keys.T
        for pair in range(PAIRS):
            lo = pair * 2 * HD
            q2 = jnp.concatenate([q_v[g, :, lo : lo + HD], q_v[g, :, lo + HD : lo + 2 * HD]], 0)
            do2 = jnp.concatenate([do_v[g, :, lo : lo + HD], do_v[g, :, lo + HD : lo + 2 * HD]], 0)
            blocks = []
            tops = []
            for d in range(SPAN):
                k_d = kv[g, 0, d * ROWS : (d + 1) * ROWS]
                if d > 0:
                    k_d = jnp.where(inside[d], k_d, jnp.zeros_like(k_d))
                s_d = dot(k_d, q2, NT)
                if d == 0:
                    s_d = jnp.where(later, -jnp.inf, s_d)
                top = jnp.max(s_d, axis=0, keepdims=True)
                if d > 0:
                    top = jnp.where(inside[d], top, -jnp.inf)
                blocks.append(s_d)
                tops.append(top)
            top = functools.reduce(jnp.maximum, tops)
            exps = []
            norm = jnp.zeros_like(top)
            for d in range(SPAN):
                top_d = top if d == 0 else jnp.where(inside[d], top, jnp.inf)
                e_d = jnp.exp2((blocks[d] - top_d) * EXP2_SCALE)
                norm = norm + jnp.sum(e_d, axis=0, keepdims=True)
                exps.append(e_d)
            inv = 1.0 / norm
            delta = jnp.zeros_like(top)
            dps = []
            for d in range(SPAN):
                p_d = exps[d] * inv
                exps[d] = p_d
                p_s[d * ROWS : (d + 1) * ROWS, lo : lo + 2 * HD] = p_d.astype(jnp.bfloat16)
                dp_d = dot(kv[g, 1, d * ROWS : (d + 1) * ROWS], do2, NT)
                delta = delta + jnp.sum(p_d * dp_d, axis=0, keepdims=True)
                dps.append(dp_d)
            for d in range(SPAN):
                ds_d = exps[d] * (dps[d] - delta)
                ds_s[d * ROWS : (d + 1) * ROWS, lo : lo + 2 * HD] = ds_d.astype(jnp.bfloat16)
        between(g)
        q6 = jnp.concatenate([q_v[g, :, j * HD : (j + 1) * HD] for j in range(PER)], 0)
        do6 = jnp.concatenate([do_v[g, :, j * HD : (j + 1) * HD] for j in range(PER)], 0)
        half = 2 * ROWS
        dk = dot(ds_s[half:], q6, NN) * INV_ROOT
        dv = dot(p_s[half:], do6, NN)
        for w, d_w in enumerate((dk, dv)):
            for d in range(2):
                terms[g, d + 1, w] = d_w[d * ROWS : (d + 1) * ROWS].astype(jnp.bfloat16)

        @pl.when(before)
        def _():
            send_pair(g).start()

        @pl.when(straight_from)
        def _():
            send_far(g).start()

        dk = dot(ds_s[:half], q6, NN) * INV_ROOT
        dv = dot(p_s[:half], do6, NN)
        for w, d_w in enumerate((dk, dv)):
            own_terms[g, w] = d_w[0:ROWS]
            terms[g, 0, w] = d_w[ROWS:half].astype(jnp.bfloat16)

        @pl.when(is_odd)
        def _():
            send_far(g).start()

    def queries_out(g):
        dq_t = dot(k_t[...], ds_s[...], NN) * INV_ROOT
        for j in range(PER):
            col = pl.multiple_of(g * WIDE + j * HD, HD)
            dq_out[:, pl.ds(col, HD)] = dq_t[:, j * HD : (j + 1) * HD].T.astype(jnp.bfloat16)

    send_cross(0)
    send_sibling(0)
    send_cross(1)
    for g in range(1, KVH):
        send_sibling(g)
    for g in range(2):
        relay(g)
        send_cross(g + 2)

    def step(g, carry):
        wait_keys(g)
        compute(g)
        queries_out(g)

        @pl.when((g > 1) & jnp.logical_not(early_sum))
        def _():
            reduce(g - 2)

        return carry

    lax.fori_loop(0, KVH, step, 0)

    @pl.when(jnp.logical_not(early_sum))
    def _():
        reduce(KVH - 2)

    reduce(KVH - 1)
    for g in range(KVH):
        finish(g)
        dk_out[:, g * HD : (g + 1) * HD] = own_terms[g, 0].astype(jnp.bfloat16)
        dv_out[:, g * HD : (g + 1) * HD] = own_terms[g, 1].astype(jnp.bfloat16)

    def drain(there, copies):
        @pl.when(there)
        def _():
            for copy in copies:
                copy.wait_send()

    drain(after, [own_cross(g) for g in range(KVH)])
    drain(is_even, [own_sibling(g) for g in range(KVH)])
    drain(relays_on, [pass_cross(g) for g in range(KVH)])
    drain(far_on, [send_far(g) for g in range(KVH)])
    drain(before, [c(g) for g in range(KVH) for c in (pass_sibling, send_pair, send_sum)])


def store_kernel(dq, dk, dv, dq_out, dk_out, dv_out, sems):
    part = ROWS // STORES
    slices = [slice(i * part, (i + 1) * part) for i in range(STORES)]
    pairs = [(dq.at[rows], dq_out.at[rows]) for rows in slices] + [(dk, dk_out), (dv, dv_out)]
    copies = [pltpu.make_async_copy(src, dst, sems.at[i]) for i, (src, dst) in enumerate(pairs)]
    for copy in copies:
        copy.start()
    for copy in copies:
        copy.wait()


def solution(mesh):
    n_ctx = mesh.shape["ctx"]
    hbm = pl.BlockSpec(memory_space=pltpu.HBM)
    vmem = pl.BlockSpec(memory_space=pltpu.VMEM)
    bf16, f32 = jnp.bfloat16, jnp.float32

    def per_device(queries, key_vectors, value_vectors, d_output, doc_blocks):
        results = pl.pallas_call(
            functools.partial(kernel, n_ctx),
            out_shape=(
                jax.ShapeDtypeStruct((ROWS, QH * HD), bf16),
                jax.ShapeDtypeStruct((ROWS, KVH * HD), bf16),
                jax.ShapeDtypeStruct((ROWS, KVH * HD), bf16),
            ),
            in_specs=[hbm] * 5,
            out_specs=(vmem, vmem, vmem),
            scratch_shapes=[
                pltpu.SMEM((NDOCS,), jnp.int32),
                pltpu.VMEM((KVH, ROWS, WIDE), bf16),
                pltpu.VMEM((KVH, ROWS, WIDE), bf16),
                pltpu.VMEM((KVH, 2, KEYS, HD), bf16),
                pltpu.VMEM((HD, KEYS), bf16),
                pltpu.VMEM((KEYS, WIDE), bf16),
                pltpu.VMEM((KEYS, WIDE), bf16),
                pltpu.VMEM((KVH, SPAN - 1, 2, ROWS, HD), bf16),
                pltpu.VMEM((KVH, 2, ROWS, HD), f32),
                pltpu.VMEM((KVH, 2, ROWS, HD), bf16),
                pltpu.VMEM((4, KVH, 2, ROWS, HD), bf16),
                pltpu.SemaphoreType.DMA,
                pltpu.SemaphoreType.DMA((KVH, 2)),
                pltpu.SemaphoreType.DMA((KVH, 2)),
                pltpu.SemaphoreType.DMA((4, KVH)),
                pltpu.SemaphoreType.DMA((SPAN, KVH)),
                pltpu.SemaphoreType.DMA((3, KVH)),
                pltpu.SemaphoreType.DMA((4, KVH)),
            ],
            compiler_params=pltpu.CompilerParams(
                collective_id=0, has_side_effects=True, vmem_limit_bytes=40 * 1024 * 1024
            ),
        )(
            *(
                pltpu.with_memory_space_constraint(x, pltpu.HBM)
                for x in (doc_blocks, queries, key_vectors, value_vectors, d_output)
            )
        )
        return pl.pallas_call(
            store_kernel,
            out_shape=[jax.ShapeDtypeStruct(x.shape, x.dtype) for x in results],
            in_specs=[vmem] * 3,
            out_specs=[hbm] * 3,
            scratch_shapes=[pltpu.SemaphoreType.DMA((STORES + 2,))],
        )(*(pltpu.with_memory_space_constraint(x, pltpu.VMEM) for x in results))

    spec = P(("dp", "ctx"), None)
    return jax.shard_map(
        per_device,
        mesh=mesh,
        in_specs=(spec, spec, spec, spec, P("dp")),
        out_specs=(spec, spec, spec),
        check_vma=False,
    )
```

```python
import functools
import math

import jax
import jax.numpy as jnp
from jax import lax
from jax.experimental import pallas as pl
from jax.experimental.pallas import tpu as pltpu
from jax.sharding import PartitionSpec as P

QH = 24
KVH = 4
HD = 128
PER = QH // KVH
ROWS = 128
SPAN = 4
NDOCS = 16
WIDE = PER * HD
PAIRS = PER // 2
INV_ROOT = 1.0 / math.sqrt(HD)
EXP2_SCALE = INV_ROOT * math.log2(math.e)
MESH = pl.DeviceIdType.MESH
NT = (((1,), (1,)), ((), ()))
NN = (((1,), (0,)), ((), ()))
KEYS = SPAN * ROWS


def dot(a, b, dims):
    return lax.dot_general(a, b, dims, preferred_element_type=jnp.float32)


def kernel(
    n_ctx,
    docs_hbm,
    q_hbm,
    k_hbm,
    v_hbm,
    do_hbm,
    dq_out,
    dk_out,
    dv_out,
    docs,
    q_v,
    do_v,
    kv,
    k_t,
    p_s,
    ds_s,
    terms,
    own_terms,
    sums,
    back,
    docs_sem,
    load_sem,
    kv_sem,
    send_sem,
    recv_sem,
    back_send,
    back_recv,
):
    me = lax.axis_index("ctx")
    core = lax.rem(me, 2)
    chip = lax.div(me, 2)
    sibling = chip * 2 + (1 - core)
    near_slot = 1 + 2 * core
    far = 3 - 2 * core

    is_even, is_odd = core == 0, core == 1
    before, after = chip >= 1, me + 2 < n_ctx
    even_before, odd_before = is_even & before, is_odd & before
    even_after, odd_after = is_even & after, is_odd & after
    relays_on = even_before & after
    straight_from, straight_to = is_even & (chip >= 2), is_odd & (me + 3 < n_ctx)

    barrier = pltpu.get_barrier_semaphore()
    partners = (
        (me >= 0, sibling),
        (even_before, me - 1),
        (odd_after, me + 1),
        (even_after, me + 3),
        (odd_before, me - 3),
        (even_after, me + 2),
        (even_before, me - 2),
        (straight_from, me - 3),
        (straight_to, me + 3),
    )
    for there, device in partners:

        @pl.when(there)
        def _():
            pl.semaphore_signal(barrier, inc=1, device_id={"ctx": device}, device_id_type=MESH)

    docs_copy = pltpu.make_async_copy(docs_hbm, docs, docs_sem)
    docs_copy.start()

    def kv_load(g, which):
        src = (k_hbm, v_hbm)[which]
        return pltpu.make_async_copy(
            src.at[:, g * HD : (g + 1) * HD], kv.at[g, which, 0:ROWS], kv_sem.at[g, which]
        )

    for g in range(KVH):
        for which in range(2):
            kv_load(g, which).start()

    def q_load(g):
        cols = slice(g * WIDE, (g + 1) * WIDE)
        return (
            pltpu.make_async_copy(q_hbm.at[:, cols], q_v.at[g], load_sem.at[g, 0]),
            pltpu.make_async_copy(do_hbm.at[:, cols], do_v.at[g], load_sem.at[g, 1]),
        )

    for g in range(KVH):
        for copy in q_load(g):
            copy.start()

    @pl.when(me < SPAN - 1)
    def _():
        for d in range(1, SPAN):

            @pl.when(me < d)
            def _():
                kv[:, :, d * ROWS : (d + 1) * ROWS] = jnp.zeros((KVH, 2, ROWS, HD), jnp.bfloat16)

    for g in range(KVH):
        for which in range(2):
            kv_load(g, which).wait()
    docs_copy.wait()

    end = jnp.int32(0)
    start = jnp.int32(0)
    for i in range(NDOCS):
        end = end + docs[i]
        start = jnp.where(end <= me, end, start)
    inside = [me - d >= start for d in range(SPAN)]

    pl.semaphore_wait(barrier, sum(there.astype(jnp.int32) for there, _ in partners))

    def kv_copy(g, from_slot, to_slot, kind, device):
        return pltpu.make_async_remote_copy(
            src_ref=kv.at[g, :, pl.ds(pl.multiple_of(from_slot * ROWS, ROWS), ROWS)],
            dst_ref=kv.at[g, :, pl.ds(pl.multiple_of(to_slot * ROWS, ROWS), ROWS)],
            send_sem=send_sem.at[kind, g],
            recv_sem=recv_sem.at[to_slot, g],
            device_id={"ctx": device},
            device_id_type=MESH,
        )

    def own_cross(g):
        return kv_copy(g, 0, far, 0, me + far)

    def own_sibling(g):
        return kv_copy(g, 0, 1, 1, sibling)

    def pass_sibling(g):
        return kv_copy(g, near_slot, 2, 2, sibling)

    def pass_cross(g):
        return kv_copy(g, 1, 3, 3, me + 2)

    def send_cross(g):
        @pl.when(after)
        def _():
            own_cross(g).start()

    def send_sibling(g):
        @pl.when(is_even)
        def _():
            own_sibling(g).start()

    def wait_slot(g, slot, there):
        @pl.when(there)
        def _():
            kv_copy(g, 0, slot, 0, sibling).wait_recv()

    def relay(g):
        @pl.when(before)
        def _():
            kv_copy(g, 0, near_slot, 0, sibling).wait_recv()

            pass_sibling(g).start()

            @pl.when(relays_on)
            def _():
                pass_cross(g).start()

    def wait_keys(g):
        wait_slot(g, 2, before)
        wait_slot(g, far, is_odd | (chip >= 2))

    def back_copy(src, slot, kind, g, device):
        return pltpu.make_async_remote_copy(
            src_ref=src,
            dst_ref=back.at[slot, g],
            send_sem=back_send.at[kind, g],
            recv_sem=back_recv.at[slot, g],
            device_id={"ctx": device},
            device_id_type=MESH,
        )

    far_on = is_odd | (chip >= 2)

    early_sum = is_odd | jnp.logical_not(straight_from & after)

    def by_chip(g):
        return (g < KVH - 1) & (is_even & (me != 4))

    def joins(g):
        return (g < KVH - 1) & (straight_from & after)

    def send_pair(g):
        return back_copy(terms.at[g, 1], 0, 0, g, sibling)

    def send_far(g):
        slot = jnp.where(by_chip(g), 3, 2)
        device = jnp.where(by_chip(g), me - 2, me - far)
        return back_copy(terms.at[g, far - 1], slot, 1, g, device)

    def send_sum(g):
        return back_copy(sums.at[g], 1, 2, g, me - near_slot)

    def wait_back(slot, g):
        back_copy(sums.at[g], slot, 2, g, sibling).wait_recv()

    def reduce(g):
        @pl.when(before)
        def _():
            wait_back(0, g)

            @pl.when(joins(g))
            def _():
                wait_back(3, g)
                for w in range(2):
                    total = terms[g, 0, w].astype(jnp.float32) + back[0, g, w].astype(jnp.float32)
                    sums[g, w] = (total + back[3, g, w].astype(jnp.float32)).astype(jnp.bfloat16)

            @pl.when(jnp.logical_not(joins(g)))
            def _():
                for w in range(2):
                    mine = terms[g, near_slot - 1, w].astype(jnp.float32)
                    sums[g, w] = (mine + back[0, g, w].astype(jnp.float32)).astype(jnp.bfloat16)

            send_sum(g).start()

    def finish(g):
        @pl.when(is_even | (straight_to & (me == 1 if g < KVH - 1 else me >= 0)))
        def _():
            wait_back(2, g)
            for w in range(2):
                own_terms[g, w] += back[2, g, w].astype(jnp.float32)

        @pl.when(after)
        def _():
            wait_back(1, g)
            for w in range(2):
                own_terms[g, w] += back[1, g, w].astype(jnp.float32)

    later = lax.broadcasted_iota(jnp.int32, (ROWS, 2 * ROWS), 0) > lax.rem(
        lax.broadcasted_iota(jnp.int32, (ROWS, 2 * ROWS), 1), ROWS
    )

    def relay_ahead(g):
        @pl.when(g < KVH - 2)
        def _():
            relay(g + 2)

    def between(g):
        @pl.when((g > 0) & early_sum)
        def _():
            reduce(g - 1)

    def compute(g):
        for which in range(2):
            pltpu.make_async_copy(
                (q_v, do_v)[which].at[g], (q_v, do_v)[which].at[g], load_sem.at[g, which]
            ).wait()
        keys = kv[g, 0]
        k_t[...] = keys.T
        for pair in range(PAIRS):
            if pair == 1:
                relay_ahead(g)
            lo = pair * 2 * HD
            q2 = jnp.concatenate([q_v[g, :, lo : lo + HD], q_v[g, :, lo + HD : lo + 2 * HD]], 0)
            do2 = jnp.concatenate([do_v[g, :, lo : lo + HD], do_v[g, :, lo + HD : lo + 2 * HD]], 0)
            blocks = []
            tops = []
            for d in range(SPAN):
                k_d = kv[g, 0, d * ROWS : (d + 1) * ROWS]
                if d > 0:
                    k_d = jnp.where(inside[d], k_d, jnp.zeros_like(k_d))
                s_d = dot(k_d, q2, NT)
                if d == 0:
                    s_d = jnp.where(later, -jnp.inf, s_d)
                top = jnp.max(s_d, axis=0, keepdims=True)
                if d > 0:
                    top = jnp.where(inside[d], top, -jnp.inf)
                blocks.append(s_d)
                tops.append(top)
            top = functools.reduce(jnp.maximum, tops)
            exps = []
            norm = jnp.zeros_like(top)
            for d in range(SPAN):
                top_d = top if d == 0 else jnp.where(inside[d], top, jnp.inf)
                e_d = jnp.exp2((blocks[d] - top_d) * EXP2_SCALE)
                norm = norm + jnp.sum(e_d, axis=0, keepdims=True)
                exps.append(e_d)
            inv = 1.0 / norm
            delta = jnp.zeros_like(top)
            dps = []
            for d in range(SPAN):
                p_d = exps[d] * inv
                exps[d] = p_d
                p_s[d * ROWS : (d + 1) * ROWS, lo : lo + 2 * HD] = p_d.astype(jnp.bfloat16)
                dp_d = dot(kv[g, 1, d * ROWS : (d + 1) * ROWS], do2, NT)
                delta = delta + jnp.sum(p_d * dp_d, axis=0, keepdims=True)
                dps.append(dp_d)
            for d in range(SPAN):
                ds_d = exps[d] * (dps[d] - delta)
                ds_s[d * ROWS : (d + 1) * ROWS, lo : lo + 2 * HD] = ds_d.astype(jnp.bfloat16)
        between(g)
        q6 = jnp.concatenate([q_v[g, :, j * HD : (j + 1) * HD] for j in range(PER)], 0)
        do6 = jnp.concatenate([do_v[g, :, j * HD : (j + 1) * HD] for j in range(PER)], 0)
        half = 2 * ROWS
        dk = dot(ds_s[half:], q6, NN) * INV_ROOT
        dv = dot(p_s[half:], do6, NN)
        for w, d_w in enumerate((dk, dv)):
            for d in range(2):
                terms[g, d + 1, w] = d_w[d * ROWS : (d + 1) * ROWS].astype(jnp.bfloat16)

        @pl.when(before)
        def _():
            send_pair(g).start()

        @pl.when(straight_from)
        def _():
            send_far(g).start()

        dk = dot(ds_s[:half], q6, NN) * INV_ROOT
        dv = dot(p_s[:half], do6, NN)
        for w, d_w in enumerate((dk, dv)):
            own_terms[g, w] = d_w[0:ROWS]
            terms[g, 0, w] = d_w[ROWS:half].astype(jnp.bfloat16)

        @pl.when(is_odd)
        def _():
            send_far(g).start()

    def queries_out(g):
        dq_t = dot(k_t[...], ds_s[...], NN) * INV_ROOT
        for j in range(PER):
            col = pl.multiple_of(g * WIDE + j * HD, HD)
            dq_out[:, pl.ds(col, HD)] = dq_t[:, j * HD : (j + 1) * HD].T.astype(jnp.bfloat16)

    send_cross(0)
    send_sibling(0)
    send_cross(1)
    for g in range(1, KVH):
        send_sibling(g)
    for g in range(2):
        relay(g)
        send_cross(g + 2)

    def step(g, carry):
        wait_keys(g)
        compute(g)
        queries_out(g)

        @pl.when((g > 1) & jnp.logical_not(early_sum))
        def _():
            reduce(g - 2)

        return carry

    lax.fori_loop(0, KVH, step, 0)

    @pl.when(jnp.logical_not(early_sum))
    def _():
        reduce(KVH - 2)

    reduce(KVH - 1)
    for g in range(KVH):
        finish(g)
        dk_out[:, g * HD : (g + 1) * HD] = own_terms[g, 0].astype(jnp.bfloat16)
        dv_out[:, g * HD : (g + 1) * HD] = own_terms[g, 1].astype(jnp.bfloat16)

    def drain(there, copies):
        @pl.when(there)
        def _():
            for copy in copies:
                copy.wait_send()

    drain(after, [own_cross(g) for g in range(KVH)])
    drain(is_even, [own_sibling(g) for g in range(KVH)])
    drain(relays_on, [pass_cross(g) for g in range(KVH)])
    drain(far_on, [send_far(g) for g in range(KVH)])
    drain(before, [c(g) for g in range(KVH) for c in (pass_sibling, send_pair, send_sum)])


def store_kernel(dq, dk, dv, dq_out, dk_out, dv_out, sems):
    copies = [
        pltpu.make_async_copy(src, dst, sems.at[i])
        for i, (src, dst) in enumerate(((dq, dq_out), (dk, dk_out), (dv, dv_out)))
    ]
    for copy in copies:
        copy.start()
    for copy in copies:
        copy.wait()


def solution(mesh):
    n_ctx = mesh.shape["ctx"]
    hbm = pl.BlockSpec(memory_space=pltpu.HBM)
    vmem = pl.BlockSpec(memory_space=pltpu.VMEM)
    bf16, f32 = jnp.bfloat16, jnp.float32

    def per_device(queries, key_vectors, value_vectors, d_output, doc_blocks):
        results = pl.pallas_call(
            functools.partial(kernel, n_ctx),
            out_shape=(
                jax.ShapeDtypeStruct((ROWS, QH * HD), bf16),
                jax.ShapeDtypeStruct((ROWS, KVH * HD), bf16),
                jax.ShapeDtypeStruct((ROWS, KVH * HD), bf16),
            ),
            in_specs=[hbm] * 5,
            out_specs=(vmem, vmem, vmem),
            scratch_shapes=[
                pltpu.SMEM((NDOCS,), jnp.int32),
                pltpu.VMEM((KVH, ROWS, WIDE), bf16),
                pltpu.VMEM((KVH, ROWS, WIDE), bf16),
                pltpu.VMEM((KVH, 2, KEYS, HD), bf16),
                pltpu.VMEM((HD, KEYS), bf16),
                pltpu.VMEM((KEYS, WIDE), bf16),
                pltpu.VMEM((KEYS, WIDE), bf16),
                pltpu.VMEM((KVH, SPAN - 1, 2, ROWS, HD), bf16),
                pltpu.VMEM((KVH, 2, ROWS, HD), f32),
                pltpu.VMEM((KVH, 2, ROWS, HD), bf16),
                pltpu.VMEM((4, KVH, 2, ROWS, HD), bf16),
                pltpu.SemaphoreType.DMA,
                pltpu.SemaphoreType.DMA((KVH, 2)),
                pltpu.SemaphoreType.DMA((KVH, 2)),
                pltpu.SemaphoreType.DMA((4, KVH)),
                pltpu.SemaphoreType.DMA((SPAN, KVH)),
                pltpu.SemaphoreType.DMA((3, KVH)),
                pltpu.SemaphoreType.DMA((4, KVH)),
            ],
            compiler_params=pltpu.CompilerParams(
                collective_id=0, has_side_effects=True, vmem_limit_bytes=40 * 1024 * 1024
            ),
        )(
            *(
                pltpu.with_memory_space_constraint(x, pltpu.HBM)
                for x in (doc_blocks, queries, key_vectors, value_vectors, d_output)
            )
        )
        return pl.pallas_call(
            store_kernel,
            out_shape=[jax.ShapeDtypeStruct(x.shape, x.dtype) for x in results],
            in_specs=[vmem] * 3,
            out_specs=[hbm] * 3,
            scratch_shapes=[pltpu.SemaphoreType.DMA((3,))],
        )(*(pltpu.with_memory_space_constraint(x, pltpu.VMEM) for x in results))

    spec = P(("dp", "ctx"), None)
    return jax.shard_map(
        per_device,
        mesh=mesh,
        in_specs=(spec, spec, spec, spec, P("dp")),
        out_specs=(spec, spec, spec),
        check_vma=False,
    )
```
